512 devices in a mesh: branch: 16 (over z_lo, y), shard: 32 (over z_hi, x, core).
Axes of the slice: x: 4, y: 4, z: 16 (z_hi: 4, z_lo: 4; z = z_hi * 4 + z_lo), core: 2. Of those that a mesh axis runs over, the one named last changes fastest.
Arguments:
- tokens: bfloat16 [2048, 4096], P('branch', 'shard'), may hold values from -45 to 45
- context: bfloat16 [2048, 2048], P('branch', 'shard'), may hold values from -6 to 6
- attn_weights: bfloat16 [16, 2048, 4096], P('branch', None, 'shard'), may hold values from -0.125 to 0.125
- norm_gain: bfloat16 [4096], P('shard'), may hold values from 0.099609375 to 1.8984375
- router: bfloat16 [4096, 16], P('shard'), may hold values from -0.375 to 0.375
- routes: int32 [2048, 2], P('branch'), may hold values from 0 to 15, all different within a row; in each aligned block of 128 rows (0 to 127, 128 to 255, ...) at most 24 rows name the same one
- gate_w: bfloat16 [16, 4096, 5632], P('branch', 'shard'), may hold values from -0.09375 to 0.09375
- up_w: bfloat16 [16, 4096, 5632], P('branch', 'shard'), may hold values from -0.09375 to 0.09375
- down_w: bfloat16 [16, 5632, 4096], P('branch', None, 'shard'), may hold values from -0.15625 to 0.15625
Outputs:
- attended: bfloat16 [2048, 4096], P('branch', 'shard')
- mixed: bfloat16 [2048, 4096], P('branch', 'shard')
The draws below stay inside these ranges and needn't reach their ends.
Inputs may be any that keep to these rules, and one draw needn't show every extreme that they name: `routes`: the two experts of a token differ; within each aligned block of 128 tokens (one group) no expert is named by more than 24 tokens, a bound that some block reaches.
All inputs are finite; a program needn't handle non-finite values.
Results may differ from the reference program's by a relative error of at most 0.03.
Values may be sent and summed in bfloat16 or wider, within the bound.
No kernel may reach another device: no remote copies, remote signals or barrier semaphores. Data moves between devices by JAX's collectives and lax.ppermute only.
A program may use at most 64 MiB of HBM per device.

```python
import math
import jax
import jax.numpy as jnp
import numpy as np
from jax import lax

D = 4096
FF = 5632
HQ = 2048
TOK_GRP = 128
EXPERTS = 16
CAP = 24
TOKENS = 2048
N_SHARD = 32


def draw_tokens(key, part):
    key = jax.random.fold_in(key, 11)
    base_key, row_key, col_key = jax.random.split(key, 3)
    position = jnp.arange(D, dtype=jnp.float32) / D
    base = jax.random.truncated_normal(base_key, -4.0, 4.0, (TOKENS, D), jnp.float32)
    lowest = math.log(0.3)
    ramp = jnp.sqrt(0.5 + position)
    row_scale = jnp.exp(jax.random.uniform(row_key, (TOKENS, 1), jnp.float32, lowest, math.log(3.0)))
    col_scale = jnp.exp(jax.random.uniform(col_key, (1, D), jnp.float32, math.log(0.3), math.log(3.0)))
    return (base * row_scale * col_scale * ramp[None, :]).astype(jnp.bfloat16)


def strengthened(values, key, source, target, shards_of, factor):
    def block_of(axis_at):
        return (jnp.arange(values.shape[axis_at]) // (values.shape[axis_at] // shards_of)).reshape((-1,) + (1,) * (values.ndim - 1 - axis_at))

    one_side = jax.random.permutation(key, shards_of)[block_of(target)]
    second = (block_of(target) + shards_of // 2) % shards_of
    return jnp.where((block_of(source) == one_side) | (block_of(source) == second), factor * values, values)


def shard_levels(own_key, shape, cuts, smallest, top_value):
    loudness, own = 1.0, jax.random.fold_in(own_key, 6)
    for axis_at, blocks in cuts:
        steps = jnp.exp(jax.random.uniform(jax.random.fold_in(own, axis_at), (blocks,), jnp.float32, smallest / len(cuts), top_value / len(cuts)))
        loudness = loudness * jnp.repeat(steps, shape[axis_at] // blocks).reshape([-1 if axis == axis_at else 1 for axis in range(len(shape))])
    return loudness


def deal_out(stream_key, own, number, rows, count, top, reach, skew):
    sequence = jax.random.permutation(stream_key, count)
    crowded, usual = load_shares(count, rows * top, reach, skew, True), load_shares(count, rows * top, reach, skew, False)
    places = jnp.arange(count)

    def named(lengths, offset_by):
        used = int((lengths > 0).sum())
        fixed = max(1, used // 4)
        passed = fixed + (places - fixed + offset_by * (used - fixed)) % max(1, count - fixed)
        return jnp.zeros((count,), jnp.int32).at[sequence[jnp.where(places < fixed, places, passed)]].set(jnp.asarray(lengths, jnp.int32))

    lengths = jnp.where(number % 4 == 0, named(crowded, number // 4), named(usual, number - number // 4 - 1))
    mixed = jax.random.permutation(jax.random.fold_in(own, 3), count)
    giver, receiver = mixed[0:count // 2 * 2:2], mixed[1:count // 2 * 2:2]
    room = jnp.minimum(lengths[giver] - 1, reach - lengths[receiver]) // 2
    room = jnp.where((giver == sequence[0]) | (receiver == sequence[0]) | (lengths[receiver] == 0), 0, jnp.maximum(room, 0))
    passed = jax.random.randint(jax.random.fold_in(own, 4), (count // 2,), 0, 1 << 20) % (room + 1)
    lengths = lengths.at[giver].add(-passed).at[receiver].add(passed)
    labels = jnp.searchsorted(jnp.cumsum(lengths), jnp.arange(rows * top), side="right").astype(jnp.int32)
    table = labels.reshape(top, rows).T
    table = table[jax.random.permutation(jax.random.fold_in(own, 1), rows)]
    offset_by = jax.random.randint(jax.random.fold_in(own, 2), (rows, 1), 0, top)
    return jnp.take_along_axis(table, (jnp.arange(top)[None, :] + offset_by) % top, axis=1)


def load_shares(amount, total, reach, slope, full):
    loads = [(1 << 20) // math.isqrt(grade ** slope) + 1 for grade in range(1, amount + 1)]
    largest = reach if full else min(reach, max(-(-total // amount), total * loads[0] // sum(loads)))
    least = 1 if total - largest >= amount - 1 else 0
    given, spare = [largest] + [least] * (amount - 1), total - largest - least * (amount - 1)
    while spare > 0:
        free = [i for i in range(1, amount) if given[i] < largest] or [i for i in range(1, amount) if given[i] < reach]
        whole, budget = sum([loads[i] for i in free]), spare
        for i in free:
            extra = min(reach - given[i], max(1, budget * loads[i] // whole), spare)
            given[i] = given[i] + extra
            spare = spare - extra
    return np.array(given)


def centred(stream_key, extent, scale, most, cuts=(), kind=jnp.bfloat16):
    level = shard_levels(stream_key, extent, cuts, -0.22, 0.18) if cuts else 1.0
    values = jax.random.normal(stream_key, extent, jnp.float32) * scale * level
    return jnp.minimum(jnp.maximum(values, -most), most).astype(kind)


def noise_with(rng, extent, scale, most, cuts, heavy, held_as=jnp.bfloat16):
    result = scale * jax.random.normal(rng, extent, jnp.float32)
    if cuts:
        result = result * shard_levels(rng, extent, cuts, -0.22, 0.18)
    return jnp.clip(strengthened(result, jax.random.fold_in(rng, 3), *heavy), -most, most).astype(held_as)


def setup_inputs(seed: int = 0) -> dict:
    key_of = jax.random.split(jax.random.key(seed), 10)
    tokens = draw_tokens(jax.random.fold_in(key_of[9], 71), 0)
    context = centred(key_of[1], (TOKENS, HQ), 1.0, 6.0, ((0, 16), (1, 32)))
    attn_weights = centred(key_of[2], (EXPERTS, HQ, D), HQ ** -0.5, 0.125, ((0, 16), (2, 32)))
    norm_gain = jnp.clip(1.0 + 0.18 * jax.random.normal(key_of[3], (D,), jnp.float32), 0.099609375, 1.8984375).astype(jnp.bfloat16)
    router = centred(key_of[4], (D, EXPERTS), (D // 16) ** -0.5, 0.375, ((0, 32),))
    routes_keys = jax.random.split(jax.random.fold_in(key_of[5], 1), TOKENS // TOK_GRP)
    routes_turns = jax.random.permutation(jax.random.fold_in(key_of[5], 3), TOKENS // TOK_GRP)
    routes = jax.vmap(lambda own, number: deal_out(jax.random.fold_in(key_of[5], 2), own, number, TOK_GRP, EXPERTS, 2, CAP, 1))(routes_keys, routes_turns).reshape((TOKENS, 2))
    gate_w = centred(key_of[6], (EXPERTS, D, FF), D ** -0.5, 0.09375, ((0, 16), (1, 32)))
    up_w = centred(key_of[7], (EXPERTS, D, FF), D ** -0.5, 0.09375, ((0, 16), (1, 32)))
    down_w = noise_with(key_of[8], (EXPERTS, FF, D), FF ** -0.5, 0.15625, ((0, 16), (2, 32)), (1, 2, 32, 2.75))
    return {"tokens": tokens, "context": context, "attn_weights": attn_weights, "norm_gain": norm_gain, "router": router, "routes": routes, "gate_w": gate_w, "up_w": up_w, "down_w": down_w}


def group_slots(group_routes, experts):
    flat = group_routes.reshape(-1)
    onehot = (flat[:, None] == jnp.arange(experts, dtype=jnp.int32)[None, :]).astype(jnp.int32)
    before = jnp.cumsum(onehot, axis=0) - onehot
    return lax.optimization_barrier(jnp.sum(before * onehot, axis=1)).reshape(group_routes.shape).astype(jnp.int32)

def reference(tokens, context, attn_weights, norm_gain, router, routes, gate_w, up_w, down_w):
    merged = (lax.optimization_barrier(jnp.sum(attn_weights.astype(jnp.float32), axis=0)) / EXPERTS).astype(jnp.bfloat16)
    attended_f = tokens.astype(jnp.float32) + jnp.dot(context, merged, preferred_element_type=jnp.float32)
    mean_square = lax.optimization_barrier(jnp.mean(attended_f * attended_f, axis=1, keepdims=True))
    normed_f = attended_f * lax.rsqrt(mean_square + 1e-05) * norm_gain.astype(jnp.float32)[None, :]
    normed = normed_f.astype(jnp.bfloat16)
    logits = jnp.dot(normed_f, router.astype(jnp.float32), precision=lax.Precision.HIGHEST)
    weights = jax.nn.sigmoid(jnp.take_along_axis(logits, routes, axis=1))
    slots = jax.vmap(lambda r: group_slots(r, EXPERTS))(routes.reshape(EXPERTS, TOK_GRP, 2)).reshape(TOKENS, 2)
    group = (jnp.arange(TOKENS, dtype=jnp.int32) // TOK_GRP)[:, None]
    places = (group * CAP + slots).astype(jnp.int32)
    spread = jnp.broadcast_to(normed[:, None, :], (TOKENS, 2, D))
    buffer = jnp.zeros((EXPERTS, EXPERTS * CAP, D), jnp.bfloat16).at[routes, places].set(spread)
    width = FF // N_SHARD

    def expert(operands):
        block, gate_m, up_m, down_m = operands
        gate = jnp.dot(block, gate_m, preferred_element_type=jnp.float32)
        up = jnp.dot(block, up_m, preferred_element_type=jnp.float32)
        hidden = (jax.nn.silu(gate) * up).astype(jnp.bfloat16)
        parts = jnp.einsum('rsf,sfd->srd', hidden.reshape(-1, N_SHARD, width).astype(jnp.float32), down_m.reshape(N_SHARD, width, D).astype(jnp.float32))
        parts = lax.optimization_barrier(parts.astype(jnp.bfloat16)).astype(jnp.float32)
        return lax.optimization_barrier(jnp.sum(parts, axis=0)).astype(jnp.bfloat16)
    outputs = lax.map(expert, (buffer, gate_w, up_w, down_w))
    picked = outputs[routes, places]
    mixed = lax.optimization_barrier(jnp.sum(picked.astype(jnp.float32) * weights[:, :, None], axis=1)).astype(jnp.bfloat16)
    return (attended_f.astype(jnp.bfloat16), mixed)
```

```python
import jax
import jax.numpy as jnp
from jax import lax
from jax.sharding import Mesh
from jax.sharding import PartitionSpec as P

D = 4096
BRANCH = ("zl", "y")
NEAR = ("x", "c")
BF = jnp.bfloat16
F32 = jnp.float32


def swap(values, axes):
    return lax.all_to_all(values, axes, split_axis=0, concat_axis=0, tiled=False)


def spread(values, axes, count):
    return swap(jnp.broadcast_to(values[None], (count,) + values.shape), axes)


def halves(values):
    high = lax.reduce_precision(values, exponent_bits=8, mantissa_bits=7)
    return high.astype(BF), (values - high).astype(BF)


def group_slots(group_routes, experts):
    flat = group_routes.reshape(-1)
    onehot = (flat[:, None] == jnp.arange(experts, dtype=jnp.int32)[None, :]).astype(jnp.int32)
    before = jnp.cumsum(onehot, axis=0) - onehot
    return jnp.sum(before * onehot, axis=1).reshape(group_routes.shape)


def body(tokens, context, attn_weights, norm_gain, router, routes, gate_w, up_w, down_w):
    experts = router.shape[1]
    token_count, width = tokens.shape
    capacity = 3 * token_count // experts
    rows = experts * capacity
    heads = attn_weights.shape[1]
    hidden_units = down_w.shape[1]
    near_units = hidden_units // 8
    own_units = near_units // 4

    gate_r = swap(gate_w[0].T.reshape(8, near_units, width), NEAR)
    up_r = swap(up_w[0].T.reshape(8, near_units, width), NEAR)
    down_r = swap(down_w[0].reshape(8, near_units, width), NEAR)

    parts = swap(attn_weights[0].reshape(experts, heads // experts, width), BRANCH)
    chunk = (jnp.sum(parts.astype(F32), axis=0) / experts).astype(BF)
    merged = spread(chunk, BRANCH, experts).reshape(heads, width)

    ctx = spread(context.T, "zh", 4)
    ctx = lax.all_gather(ctx, NEAR, axis=1, tiled=False).reshape(heads, token_count)
    attention_out = lax.dot_general(ctx, merged, (((0,), (0,)), ((), ())), preferred_element_type=F32)
    attended_f = tokens.astype(F32) + attention_out
    gained_f = attended_f * norm_gain.astype(F32)[None, :]
    squares = jnp.sum(attended_f * attended_f, axis=1, keepdims=True)
    scores = jnp.dot(gained_f, router.astype(F32), precision=lax.Precision.HIGHEST)

    places = routes * capacity + group_slots(routes, experts)
    table = jnp.any(
        jnp.arange(rows, dtype=jnp.int32)[:, None, None] == places[None, :, :], axis=2
    ).astype(BF)
    sent = jnp.dot(table, gained_f.astype(BF), preferred_element_type=F32).astype(BF)
    high, low = halves(jnp.concatenate([squares, scores], axis=1))
    extra = jnp.dot(table, jnp.concatenate([high, low], axis=1), preferred_element_type=F32)
    extra = extra.reshape(experts, capacity, 2, 1 + experts)
    own = jnp.eye(experts, dtype=F32)[:, None, None, :]
    score_part = jnp.sum(extra[..., 1:] * own, axis=3)
    extra = jnp.concatenate([extra[..., 0], score_part], axis=2).transpose(0, 2, 1).astype(BF)
    extra = jnp.pad(extra, ((0, 0), (0, 4), (0, width - capacity)))
    sent = jnp.concatenate([sent.reshape(experts, capacity, width), extra], axis=1)
    received = swap(sent, BRANCH)
    near = lax.all_gather(received, NEAR, axis=0, tiled=False)
    piece = near[:, :, :capacity].reshape(8, rows, width)
    extra = jnp.sum(near[:, :, capacity : capacity + 4, :capacity].astype(F32), axis=0)
    extra = extra.transpose(1, 0, 2).reshape(4, rows)
    extra_high, extra_low = halves(jnp.stack([extra[0] + extra[1], extra[2] + extra[3]]))
    extra = jnp.concatenate([extra_high, extra_low, jnp.zeros((12, rows), BF)])

    product = (((0, 2), (0, 2)), ((), ()))
    gate = lax.dot_general(gate_r, piece, product, preferred_element_type=F32).astype(BF)
    up = lax.dot_general(up_r, piece, product, preferred_element_type=F32).astype(BF)
    partial = jnp.concatenate(
        [
            gate.reshape(4, own_units, rows),
            up.reshape(4, own_units, rows),
            jnp.broadcast_to(extra[None], (4, 16, rows)),
        ],
        axis=1,
    )
    total = jnp.sum(swap(partial, "zh").astype(F32), axis=0)
    square_sum = total[2 * own_units] + total[2 * own_units + 2]
    score = total[2 * own_units + 1] + total[2 * own_units + 3]
    scale = lax.rsqrt(square_sum / D + 1e-05)
    weight = jax.nn.sigmoid(score * scale)
    gate = total[:own_units] * scale[None, :]
    up = total[own_units : 2 * own_units] * scale[None, :]
    hidden = (jax.nn.silu(gate) * up).astype(BF)
    hidden = lax.all_gather(hidden, "zh", axis=0, tiled=True)

    terms = lax.dot_general(
        hidden, down_r, (((0,), (1,)), ((), ())), preferred_element_type=F32
    ).astype(BF)
    terms = swap(terms.transpose(1, 0, 2), NEAR)
    expert_out = jnp.sum(terms.astype(F32), axis=0)
    expert_out = (expert_out * weight[:, None]).astype(BF)
    returned = swap(expert_out.reshape(experts, capacity, width), BRANCH).reshape(rows, width)
    mixed = lax.dot_general(table, returned, (((0,), (0,)), ((), ())), preferred_element_type=F32)
    return (attended_f.astype(BF), mixed.astype(BF))


def solution(mesh):
    fine = Mesh(mesh.devices.reshape(4, 4, 4, 4, 2), ("zl", "y", "zh", "x", "c"))
    shard = ("zh", "x", "c")
    in_specs = (
        P(BRANCH, shard),
        P(BRANCH, shard),
        P(BRANCH, None, shard),
        P(shard),
        P(shard, None),
        P(BRANCH, None),
        P(BRANCH, shard, None),
        P(BRANCH, shard, None),
        P(BRANCH, None, shard),
    )
    out_specs = (P(BRANCH, shard), P(BRANCH, shard))
    return jax.shard_map(body, mesh=fine, in_specs=in_specs, out_specs=out_specs, check_vma=False)
```

```python
import jax
import jax.numpy as jnp
from jax import lax
from jax.sharding import Mesh
from jax.sharding import PartitionSpec as P

D = 4096
BRANCH = ("zl", "y")
NEAR = ("x", "c")
BF = jnp.bfloat16
F32 = jnp.float32


def swap(values, axes):
    return lax.all_to_all(values, axes, split_axis=0, concat_axis=0, tiled=False)


def spread(values, axes, count):
    return swap(jnp.broadcast_to(values[None], (count,) + values.shape), axes)


def at(values, index):
    return lax.dynamic_index_in_dim(values, index, 0, keepdims=False)


def shift(values, axis, step, count):
    return lax.ppermute(values, axis, [(i, (i + step) % count) for i in range(count)])


def add(*terms):
    total = terms[0].astype(F32)
    for term in terms[1:]:
        total = total + term.astype(F32)
    return total


def pair_up(blocks):
    core = lax.axis_index("c")
    kept = lax.dynamic_index_in_dim(blocks, core, 1, keepdims=False)
    other = lax.dynamic_index_in_dim(blocks, 1 - core, 1, keepdims=False)
    return jnp.stack([kept, shift(other, "c", 1, 2)], axis=1)


def relay_x(both):
    x = lax.axis_index("x")
    return [at(both, x)] + [shift(at(both, (x + k) % 4), "x", k, 4) for k in (1, 2, 3)]


def in_order(relaid):
    x, core = lax.axis_index("x"), lax.axis_index("c")
    held = jnp.zeros((8,) + relaid[0].shape[1:], relaid[0].dtype)
    for k in range(4):
        for j in range(2):
            sender = 2 * ((x + 4 - k) % 4) + (core + j) % 2
            held = lax.dynamic_update_index_in_dim(held, relaid[k][j], sender, 0)
    return held


def add(*terms):
    total = terms[0].astype(F32)
    for term in terms[1:]:
        total = total + term.astype(F32)
    return total


def pair_up(blocks):
    core = lax.axis_index("c")
    kept = lax.dynamic_index_in_dim(blocks, core, 1, keepdims=False)
    other = lax.dynamic_index_in_dim(blocks, 1 - core, 1, keepdims=False)
    return jnp.stack([kept, shift(other, "c", 1, 2)], axis=1)


def relay_x(both):
    x = lax.axis_index("x")
    return [at(both, x)] + [shift(at(both, (x + k) % 4), "x", k, 4) for k in (1, 2, 3)]


def gather_far(values):
    z = lax.axis_index("zh")
    held = jnp.zeros((4,) + values.shape, values.dtype)
    for k in range(4):
        came = shift(values, "zh", k, 4) if k else values
        held = lax.dynamic_update_index_in_dim(held, came, (z + 4 - k) % 4, 0)
    return held


def sum_far(gate, up):
    z = lax.axis_index("zh")
    g = [at(gate, (z + k) % 4) for k in range(4)]
    u = [at(up, (z + k) % 4) for k in range(4)]
    n, m = g[0].shape[0], u[0].shape[0]
    ahead = shift(jnp.concatenate([g[2], u[1]]), "zh", 1, 4)
    back = shift(jnp.concatenate([u[2], g[3]]), "zh", 3, 4)
    ahead_two = shift(add(g[1], ahead[:n]).astype(BF), "zh", 1, 4)
    back_two = shift(add(u[3], back[:m]).astype(BF), "zh", 3, 4)
    return add(g[0], back[m:], ahead_two), add(u[0], ahead[n:], back_two)


def halves(values):
    high = lax.reduce_precision(values, exponent_bits=8, mantissa_bits=7)
    return high.astype(BF), (values - high).astype(BF)


def group_slots(group_routes, experts):
    flat = group_routes.reshape(-1)
    onehot = (flat[:, None] == jnp.arange(experts, dtype=jnp.int32)[None, :]).astype(jnp.int32)
    before = jnp.cumsum(onehot, axis=0) - onehot
    return jnp.sum(before * onehot, axis=1).reshape(group_routes.shape)


def body(tokens, context, attn_weights, norm_gain, router, routes, gate_w, up_w, down_w):
    experts = router.shape[1]
    token_count, width = tokens.shape
    capacity = 3 * token_count // experts
    rows = experts * capacity
    heads = attn_weights.shape[1]
    hidden_units = down_w.shape[1]
    near_units = hidden_units // 8
    own_units = near_units // 4

    blocks = jnp.concatenate(
        [
            gate_w[0].T.reshape(4, 2, near_units, width),
            up_w[0].T.reshape(4, 2, near_units, width),
        ],
        axis=2,
    )
    both = pair_up(blocks)

    parts = swap(attn_weights[0].reshape(experts, heads // experts, width), BRANCH)
    chunk = (jnp.sum(parts.astype(F32), axis=0) / experts).astype(BF)
    relaid = relay_x(both)
    ctx = lax.all_gather(context.T, "zh", axis=0, tiled=False)
    chunk, ctx, relaid[1], relaid[3] = lax.optimization_barrier((chunk, ctx, relaid[1], relaid[3]))
    merged = spread(chunk, BRANCH, experts).reshape(heads, width)
    merged, relaid[2] = lax.optimization_barrier((merged, relaid[2]))

    ctx = lax.all_gather(ctx, NEAR, axis=1, tiled=False).reshape(heads, token_count)
    attention_out = lax.dot_general(ctx, merged, (((0,), (0,)), ((), ())), preferred_element_type=F32)
    attended_f = tokens.astype(F32) + attention_out
    gained_f = attended_f * norm_gain.astype(F32)[None, :]
    squares = jnp.sum(attended_f * attended_f, axis=1, keepdims=True)
    scores = jnp.dot(gained_f, router.astype(F32), precision=lax.Precision.HIGHEST)

    places = routes * capacity + group_slots(routes, experts)
    table = jnp.any(
        jnp.arange(rows, dtype=jnp.int32)[:, None, None] == places[None, :, :], axis=2
    ).astype(BF)
    sent = jnp.dot(table, gained_f.astype(BF), preferred_element_type=F32).astype(BF)
    high, low = halves(jnp.concatenate([squares, scores], axis=1))
    extra = jnp.dot(table, jnp.concatenate([high, low], axis=1), preferred_element_type=F32)
    extra = extra.reshape(experts, capacity, 2, 1 + experts)
    own = jnp.eye(experts, dtype=F32)[:, None, None, :]
    score_part = jnp.sum(extra[..., 1:] * own, axis=3)
    extra = jnp.concatenate([extra[..., 0], score_part], axis=2).transpose(0, 2, 1).astype(BF)
    extra = jnp.pad(extra.reshape(experts, 1, 4 * capacity), ((0, 0), (0, 0), (0, width - 4 * capacity)))
    sent = jnp.concatenate([sent.reshape(experts, capacity, width), extra], axis=1)
    received = swap(sent, BRANCH)
    received = jnp.concatenate([received[:, :capacity].reshape(rows, width), received[:, capacity]])
    received, weights = lax.optimization_barrier((received, in_order(relaid)))
    near = lax.all_gather(received, NEAR, axis=0, tiled=False)
    extra = jnp.sum(near[:, rows:, : 4 * capacity].astype(F32), axis=0)
    extra = extra.reshape(experts, 4, capacity).transpose(1, 0, 2).reshape(4, rows)
    extra_high, extra_low = halves(jnp.stack([extra[0] + extra[1], extra[2] + extra[3]]))
    extra = jnp.concatenate([extra_high, extra_low, jnp.zeros((12, rows), BF)])

    down_blocks, near = lax.optimization_barrier((down_w[0], near))
    down_r = swap(down_blocks.reshape(8, near_units, width), NEAR)

    product = lax.dot_general(
        weights, near, (((0, 2), (0, 2)), ((), ())), preferred_element_type=F32
    )
    product = product[:, :rows].astype(BF).reshape(2, 4, own_units, rows)
    extra = jnp.broadcast_to(extra[None], (4, 16, rows))
    gate, up = sum_far(product[0], jnp.concatenate([product[1], extra], axis=1))
    square_sum = up[own_units] + up[own_units + 2]
    score = up[own_units + 1] + up[own_units + 3]
    scale = lax.rsqrt(square_sum / D + 1e-05)
    weight = jax.nn.sigmoid(score * scale)
    gate = gate * scale[None, :]
    up = up[:own_units] * scale[None, :]
    hidden = (jax.nn.silu(gate) * up).astype(BF)
    hidden = lax.all_gather(hidden, "zh", axis=0, tiled=True)

    terms = lax.dot_general(
        hidden, down_r, (((0,), (1,)), ((), ())), preferred_element_type=F32
    ).astype(BF)
    terms = swap(terms.transpose(1, 0, 2), NEAR)
    expert_out = jnp.sum(terms.astype(F32), axis=0)
    expert_out = (expert_out * weight[:, None]).astype(BF)
    returned = swap(expert_out.reshape(experts, capacity, width), BRANCH).reshape(rows, width)
    mixed = lax.dot_general(table, returned, (((0,), (0,)), ((), ())), preferred_element_type=F32)
    return (attended_f.astype(BF), mixed.astype(BF))


def solution(mesh):
    fine = Mesh(mesh.devices.reshape(4, 4, 4, 4, 2), ("zl", "y", "zh", "x", "c"))
    shard = ("zh", "x", "c")
    in_specs = (
        P(BRANCH, shard),
        P(BRANCH, shard),
        P(BRANCH, None, shard),
        P(shard),
        P(shard, None),
        P(BRANCH, None),
        P(BRANCH, shard, None),
        P(BRANCH, shard, None),
        P(BRANCH, None, shard),
    )
    out_specs = (P(BRANCH, shard), P(BRANCH, shard))
    return jax.shard_map(body, mesh=fine, in_specs=in_specs, out_specs=out_specs, check_vma=False)
```

```python
import jax
import jax.numpy as jnp
from jax import lax
from jax.sharding import Mesh
from jax.sharding import PartitionSpec as P

D = 4096
BRANCH = ("zl", "y")
NEAR = ("x", "c")
BF = jnp.bfloat16
F32 = jnp.float32


def swap(values, axes):
    return lax.all_to_all(values, axes, split_axis=0, concat_axis=0, tiled=False)


def spread(values, axes, count):
    return swap(jnp.broadcast_to(values[None], (count,) + values.shape), axes)


def at(values, index):
    return lax.dynamic_index_in_dim(values, index, 0, keepdims=False)


def shift(values, axis, step, count):
    return lax.ppermute(values, axis, [(i, (i + step) % count) for i in range(count)])


def add(*terms):
    total = terms[0].astype(F32)
    for term in terms[1:]:
        total = total + term.astype(F32)
    return total


def pair_up(blocks):
    core = lax.axis_index("c")
    kept = lax.dynamic_index_in_dim(blocks, core, 1, keepdims=False)
    other = lax.dynamic_index_in_dim(blocks, 1 - core, 1, keepdims=False)
    return jnp.stack([kept, shift(other, "c", 1, 2)], axis=1)


def relay_x(both):
    x = lax.axis_index("x")
    return [at(both, x)] + [shift(at(both, (x + k) % 4), "x", k, 4) for k in (1, 2, 3)]


def in_order(relaid):
    x, core = lax.axis_index("x"), lax.axis_index("c")
    held = jnp.zeros((8,) + relaid[0].shape[1:], relaid[0].dtype)
    for k in range(4):
        for j in range(2):
            sender = 2 * ((x + 4 - k) % 4) + (core + j) % 2
            held = lax.dynamic_update_index_in_dim(held, relaid[k][j], sender, 0)
    return held


def add(*terms):
    total = terms[0].astype(F32)
    for term in terms[1:]:
        total = total + term.astype(F32)
    return total


def pair_up(blocks):
    core = lax.axis_index("c")
    kept = lax.dynamic_index_in_dim(blocks, core, 1, keepdims=False)
    other = lax.dynamic_index_in_dim(blocks, 1 - core, 1, keepdims=False)
    return jnp.stack([kept, shift(other, "c", 1, 2)], axis=1)


def relay_x(both):
    x = lax.axis_index("x")
    return [at(both, x)] + [shift(at(both, (x + k) % 4), "x", k, 4) for k in (1, 2, 3)]


def sum_far(gate, up):
    z = lax.axis_index("zh")
    g = [at(gate, (z + k) % 4) for k in range(4)]
    u = [at(up, (z + k) % 4) for k in range(4)]
    n, m = g[0].shape[0], u[0].shape[0]
    ahead = shift(jnp.concatenate([g[2], u[1]]), "zh", 1, 4)
    back = shift(jnp.concatenate([u[2], g[3]]), "zh", 3, 4)
    ahead_two = shift(add(g[1], ahead[:n]).astype(BF), "zh", 1, 4)
    back_two = shift(add(u[3], back[:m]).astype(BF), "zh", 3, 4)
    return add(g[0], back[m:], ahead_two), add(u[0], ahead[n:], back_two)


def halves(values):
    high = lax.reduce_precision(values, exponent_bits=8, mantissa_bits=7)
    return high.astype(BF), (values - high).astype(BF)


def group_slots(group_routes, experts):
    flat = group_routes.reshape(-1)
    pairs = jnp.arange(flat.shape[0], dtype=jnp.int32)
    onehot = (flat[:, None] == jnp.arange(experts, dtype=jnp.int32)[None, :]).astype(BF)
    earlier = (pairs[:, None] > pairs[None, :]).astype(BF)
    before = jnp.dot(earlier, onehot, preferred_element_type=F32)
    slots = jnp.sum(before * onehot.astype(F32), axis=1)
    return slots.astype(jnp.int32).reshape(group_routes.shape)


def body(tokens, context, attn_weights, norm_gain, router, routes, gate_w, up_w, down_w):
    experts = router.shape[1]
    token_count, width = tokens.shape
    capacity = 3 * token_count // experts
    rows = experts * capacity
    heads = attn_weights.shape[1]
    hidden_units = down_w.shape[1]
    near_units = hidden_units // 8
    own_units = near_units // 4

    blocks = jnp.concatenate(
        [
            gate_w[0].T.reshape(4, 2, near_units, width),
            up_w[0].T.reshape(4, 2, near_units, width),
        ],
        axis=2,
    )
    both = pair_up(blocks)

    parts = swap(attn_weights[0].reshape(experts, heads // experts, width), BRANCH)
    chunk = (jnp.sum(parts.astype(F32), axis=0) / experts).astype(BF)
    relaid = relay_x(both)
    ctx = lax.all_gather(context.T, "zh", axis=0, tiled=False)
    chunk, ctx, relaid[1], relaid[3] = lax.optimization_barrier((chunk, ctx, relaid[1], relaid[3]))
    merged = spread(chunk, BRANCH, experts).reshape(heads, width)
    merged, relaid[2] = lax.optimization_barrier((merged, relaid[2]))

    ctx = lax.all_gather(ctx, NEAR, axis=1, tiled=False).reshape(heads, token_count)
    attention_out = lax.dot_general(ctx, merged, (((0,), (0,)), ((), ())), preferred_element_type=F32)
    attended_f = tokens.astype(F32) + attention_out
    gained_f = attended_f * norm_gain.astype(F32)[None, :]
    squares = jnp.sum(attended_f * attended_f, axis=1, keepdims=True)
    scores = jnp.dot(gained_f, router.astype(F32), precision=lax.Precision.HIGHEST)

    places = routes * capacity + group_slots(routes, experts)
    table = jnp.any(
        jnp.arange(rows, dtype=jnp.int32)[:, None, None] == places[None, :, :], axis=2
    ).astype(BF)
    sent = jnp.dot(table, gained_f.astype(BF), preferred_element_type=F32).astype(BF)
    high, low = halves(jnp.concatenate([squares, scores], axis=1))
    extra = jnp.dot(table, jnp.concatenate([high, low], axis=1), preferred_element_type=F32)
    extra = extra.reshape(experts, capacity, 2, 1 + experts)
    own = jnp.eye(experts, dtype=F32)[:, None, None, :]
    score_part = jnp.sum(extra[..., 1:] * own, axis=3)
    extra = jnp.concatenate([extra[..., 0], score_part], axis=2).transpose(0, 2, 1).astype(BF)
    extra = jnp.pad(extra.reshape(experts, 1, 4 * capacity), ((0, 0), (0, 0), (0, width - 4 * capacity)))
    sent = jnp.concatenate([sent.reshape(experts, capacity, width), extra], axis=1)
    received = swap(sent, BRANCH)
    received = jnp.concatenate([received[:, :capacity].reshape(rows, width), received[:, capacity]])
    received, weights = lax.optimization_barrier((received, in_order(relaid)))
    near = lax.all_gather(received, NEAR, axis=0, tiled=False)
    extra = jnp.sum(near[:, rows:, : 4 * capacity].astype(F32), axis=0)
    extra = extra.reshape(experts, 4, capacity).transpose(1, 0, 2).reshape(4, rows)
    extra_high, extra_low = halves(jnp.stack([extra[0] + extra[1], extra[2] + extra[3]]))
    extra = jnp.concatenate([extra_high, extra_low, jnp.zeros((4, rows), BF)])

    down_blocks, near = lax.optimization_barrier((down_w[0], near))
    down_r = swap(down_blocks.reshape(8, near_units, width), NEAR)

    product = lax.dot_general(
        weights, near, (((0, 2), (0, 2)), ((), ())), preferred_element_type=F32
    )
    product = product[:, :rows].astype(BF).reshape(2, 4, own_units, rows)
    extra = jnp.broadcast_to(extra[None], (4, 8, rows))
    gate, up = sum_far(product[0], jnp.concatenate([product[1], extra], axis=1))
    square_sum = up[own_units] + up[own_units + 2]
    score = up[own_units + 1] + up[own_units + 3]
    scale = lax.rsqrt(square_sum / D + 1e-05)
    weight = jax.nn.sigmoid(score * scale)
    gate = gate * scale[None, :]
    up = up[:own_units] * scale[None, :]
    hidden = (jax.nn.silu(gate) * up).astype(BF)
    hidden = lax.all_gather(hidden, "zh", axis=0, tiled=True)

    terms = lax.dot_general(
        hidden, down_r, (((0,), (1,)), ((), ())), preferred_element_type=F32
    ).astype(BF)
    terms = swap(terms.transpose(1, 0, 2), NEAR)
    expert_out = jnp.sum(terms.astype(F32), axis=0)
    expert_out = (expert_out * weight[:, None]).astype(BF)
    returned = swap(expert_out.reshape(experts, capacity, width), BRANCH).reshape(rows, width)
    mixed = lax.dot_general(table, returned, (((0,), (0,)), ((), ())), preferred_element_type=F32)
    return (attended_f.astype(BF), mixed.astype(BF))


def solution(mesh):
    fine = Mesh(mesh.devices.reshape(4, 4, 4, 4, 2), ("zl", "y", "zh", "x", "c"))
    shard = ("zh", "x", "c")
    in_specs = (
        P(BRANCH, shard),
        P(BRANCH, shard),
        P(BRANCH, None, shard),
        P(shard),
        P(shard, None),
        P(BRANCH, None),
        P(BRANCH, shard, None),
        P(BRANCH, shard, None),
        P(BRANCH, None, shard),
    )
    out_specs = (P(BRANCH, shard), P(BRANCH, shard))
    return jax.shard_map(body, mesh=fine, in_specs=in_specs, out_specs=out_specs, check_vma=False)
```

```python
import jax
import jax.numpy as jnp
from jax import lax
from jax.sharding import Mesh
from jax.sharding import PartitionSpec as P

D = 4096
BRANCH = ("zl", "y")
NEAR = ("x", "c")
BF = jnp.bfloat16
F32 = jnp.float32


def swap(values, axes):
    return lax.all_to_all(values, axes, split_axis=0, concat_axis=0, tiled=False)


def spread(values, axes, count):
    return swap(jnp.broadcast_to(values[None], (count,) + values.shape), axes)


def at(values, index):
    return lax.dynamic_index_in_dim(values, index, 0, keepdims=False)


def shift(values, axis, step, count):
    return lax.ppermute(values, axis, [(i, (i + step) % count) for i in range(count)])


def add(*terms):
    total = terms[0].astype(F32)
    for term in terms[1:]:
        total = total + term.astype(F32)
    return total


def pair_up(blocks):
    core = lax.axis_index("c")
    kept = lax.dynamic_index_in_dim(blocks, core, 1, keepdims=False)
    other = lax.dynamic_index_in_dim(blocks, 1 - core, 1, keepdims=False)
    return jnp.stack([kept, shift(other, "c", 1, 2)], axis=1)


def relay_x(both):
    x = lax.axis_index("x")
    return [at(both, x)] + [shift(at(both, (x + k) % 4), "x", k, 4) for k in (1, 2, 3)]


def in_order(relaid):
    x, core = lax.axis_index("x"), lax.axis_index("c")
    held = jnp.zeros((8,) + relaid[0].shape[1:], relaid[0].dtype)
    for k in range(4):
        for j in range(2):
            sender = 2 * ((x + 4 - k) % 4) + (core + j) % 2
            held = lax.dynamic_update_index_in_dim(held, relaid[k][j], sender, 0)
    return held


def shift_far(values, step):
    pairs = [(2 * z + c, 2 * ((z + step * (1 - 2 * c)) % 4) + c) for z in range(4) for c in range(2)]
    return lax.ppermute(values, ("zh", "c"), pairs)


def sum_far(gate, up):
    z, turn = lax.axis_index("zh"), 1 + 2 * lax.axis_index("c")
    g = [at(gate, (z + turn * k) % 4) for k in range(4)]
    u = [at(up, (z + turn * k) % 4) for k in range(4)]
    n, m = g[0].shape[0], u[0].shape[0]
    first, second = shift_far(g[2], 1), shift_far(u[2], -1)
    ahead = shift_far(jnp.concatenate([add(g[1], first).astype(BF), u[1]]), 1)
    back = shift_far(jnp.concatenate([add(u[3], second).astype(BF), g[3]]), -1)
    return add(g[0], back[m:], ahead[:n]), add(u[0], ahead[n:], back[:m])


def halves(values):
    high = lax.reduce_precision(values, exponent_bits=8, mantissa_bits=7)
    return high.astype(BF), (values - high).astype(BF)


def group_slots(group_routes, experts):
    flat = group_routes.reshape(-1)
    pairs = jnp.arange(flat.shape[0], dtype=jnp.int32)
    onehot = (flat[:, None] == jnp.arange(experts, dtype=jnp.int32)[None, :]).astype(BF)
    earlier = (pairs[:, None] > pairs[None, :]).astype(BF)
    before = jnp.dot(earlier, onehot, preferred_element_type=F32)
    slots = jnp.sum(before * onehot.astype(F32), axis=1)
    return slots.astype(jnp.int32).reshape(group_routes.shape)


def body(tokens, context, attn_weights, norm_gain, router, routes, gate_w, up_w, down_w):
    experts = router.shape[1]
    token_count, width = tokens.shape
    capacity = 3 * token_count // experts
    rows = experts * capacity
    heads = attn_weights.shape[1]
    hidden_units = down_w.shape[1]
    near_units = hidden_units // 8
    own_units = near_units // 4

    blocks = jnp.concatenate(
        [
            gate_w[0].T.reshape(4, 2, near_units, width),
            up_w[0].T.reshape(4, 2, near_units, width),
        ],
        axis=2,
    )
    both = pair_up(blocks)

    parts = swap(attn_weights[0].reshape(experts, heads // experts, width), BRANCH)
    chunk = (jnp.sum(parts.astype(F32), axis=0) / experts).astype(BF)
    relaid = relay_x(both)
    ctx = lax.all_gather(context.T, "zh", axis=0, tiled=False)
    chunk, ctx, relaid[1], relaid[3] = lax.optimization_barrier((chunk, ctx, relaid[1], relaid[3]))
    merged = spread(chunk, BRANCH, experts).reshape(heads, width)
    merged, relaid[2] = lax.optimization_barrier((merged, relaid[2]))

    ctx = lax.all_gather(ctx, NEAR, axis=1, tiled=False).reshape(heads, token_count)
    attention_out = lax.dot_general(ctx, merged, (((0,), (0,)), ((), ())), preferred_element_type=F32)
    attended_f = tokens.astype(F32) + attention_out
    gained_f = attended_f * norm_gain.astype(F32)[None, :]
    squares = jnp.sum(attended_f * attended_f, axis=1, keepdims=True)
    scores = jnp.dot(gained_f, router.astype(F32), precision=lax.Precision.HIGHEST)

    places = routes * capacity + group_slots(routes, experts)
    table = jnp.any(
        jnp.arange(rows, dtype=jnp.int32)[:, None, None] == places[None, :, :], axis=2
    ).astype(BF)
    sent = jnp.dot(table, gained_f.astype(BF), preferred_element_type=F32).astype(BF)
    high, low = halves(jnp.concatenate([squares, scores], axis=1))
    extra = jnp.dot(table, jnp.concatenate([high, low], axis=1), preferred_element_type=F32)
    extra = extra.reshape(experts, capacity, 2, 1 + experts)
    own = jnp.eye(experts, dtype=F32)[:, None, None, :]
    score_part = jnp.sum(extra[..., 1:] * own, axis=3)
    extra = jnp.concatenate([extra[..., 0], score_part], axis=2).transpose(0, 2, 1).astype(BF)
    extra = jnp.pad(extra.reshape(experts, 1, 4 * capacity), ((0, 0), (0, 0), (0, width - 4 * capacity)))
    sent = jnp.concatenate([sent.reshape(experts, capacity, width), extra], axis=1)
    received = swap(sent, BRANCH)
    received = jnp.concatenate([received[:, :capacity].reshape(rows, width), received[:, capacity]])
    received, weights = lax.optimization_barrier((received, in_order(relaid)))
    near = lax.all_gather(received, NEAR, axis=0, tiled=False)
    extra = jnp.sum(near[:, rows:, : 4 * capacity].astype(F32), axis=0)
    extra = extra.reshape(experts, 4, capacity).transpose(1, 0, 2).reshape(4, rows)
    extra_high, extra_low = halves(jnp.stack([extra[0] + extra[1], extra[2] + extra[3]]))
    extra = jnp.concatenate([extra_high, extra_low, jnp.zeros((4, rows), BF)])

    down_blocks, near = lax.optimization_barrier((down_w[0], near))
    down_r = swap(down_blocks.reshape(8, near_units, width), NEAR)

    product = lax.dot_general(
        weights, near, (((0, 2), (0, 2)), ((), ())), preferred_element_type=F32
    )
    product = product[:, :rows].astype(BF).reshape(2, 4, own_units, rows)
    extra = jnp.broadcast_to(extra[None], (4, 8, rows))
    gate, up = sum_far(product[0], jnp.concatenate([product[1], extra], axis=1))
    square_sum = up[own_units] + up[own_units + 2]
    score = up[own_units + 1] + up[own_units + 3]
    scale = lax.rsqrt(square_sum / D + 1e-05)
    weight = jax.nn.sigmoid(score * scale)
    gate = gate * scale[None, :]
    up = up[:own_units] * scale[None, :]
    hidden = (jax.nn.silu(gate) * up).astype(BF)
    hidden = lax.all_gather(hidden, "zh", axis=0, tiled=True)

    terms = lax.dot_general(
        hidden, down_r, (((0,), (1,)), ((), ())), preferred_element_type=F32
    ).astype(BF)
    terms = swap(terms.transpose(1, 0, 2), NEAR)
    expert_out = jnp.sum(terms.astype(F32), axis=0)
    expert_out = (expert_out * weight[:, None]).astype(BF)
    returned = swap(expert_out.reshape(experts, capacity, width), BRANCH).reshape(rows, width)
    mixed = lax.dot_general(table, returned, (((0,), (0,)), ((), ())), preferred_element_type=F32)
    return (attended_f.astype(BF), mixed.astype(BF))


def solution(mesh):
    fine = Mesh(mesh.devices.reshape(4, 4, 4, 4, 2), ("zl", "y", "zh", "x", "c"))
    shard = ("zh", "x", "c")
    in_specs = (
        P(BRANCH, shard),
        P(BRANCH, shard),
        P(BRANCH, None, shard),
        P(shard),
        P(shard, None),
        P(BRANCH, None),
        P(BRANCH, shard, None),
        P(BRANCH, shard, None),
        P(BRANCH, None, shard),
    )
    out_specs = (P(BRANCH, shard), P(BRANCH, shard))
    return jax.shard_map(body, mesh=fine, in_specs=in_specs, out_specs=out_specs, check_vma=False)
```
